512 devices in a mesh: narrow: 16 (over x, z_hi), wide: 32 (over y, z_lo, core).
Axes of the slice: x: 4, y: 8, z: 8 (z_hi: 4, z_lo: 2; z = z_hi * 2 + z_lo), core: 2. Of those that a mesh axis runs over, the one named last changes fastest.
Arguments:
- vertex: float32 [16, 32, 512, 128], P('narrow', 'wide'), may hold values from -2 to 2
- vertex_state: float32 [16, 32, 512], P('narrow', 'wide'), may hold values from 0.05 to 1
- context: float32 [16, 32, 512, 128], P('narrow', 'wide'), may hold values from -2 to 2
- context_state: float32 [16, 32, 512], P('narrow', 'wide'), may hold values from 0.05 to 1
- hub: float32 [32, 2048, 128], P('wide'), may hold values from -2 to 2
- hub_state: float32 [32, 2048], P('wide'), may hold values from 0.05 to 1
- edge_src: int32 [16, 32, 2, 1024], P('narrow', 'wide'), may hold values from 0 to 511
- edge_ctx: int32 [16, 32, 2, 1024], P('narrow', 'wide'), may hold values from 0 to 2559, as said below
- negatives: int32 [16, 32, 2, 2, 1024], P('narrow', 'wide'), may hold values from 0 to 511
- counts: int32 [16, 32, 2], P('narrow', 'wide'), may hold values from 128 to 1024, as said below
Outputs:
- vertex_out: float32 [16, 32, 512, 128], P('narrow', 'wide')
- vertex_state_out: float32 [16, 32, 512], P('narrow', 'wide')
- context_out: float32 [16, 32, 512, 128], P('narrow', 'wide')
- context_state_out: float32 [16, 32, 512], P('narrow', 'wide')
- hub_out: float32 [32, 2048, 128], P('wide')
- hub_state_out: float32 [32, 2048], P('wide')
The draws below stay inside these ranges and needn't reach their ends.
Inputs may be any that keep to these rules, and one draw needn't show every extreme that they name: `edge_ctx`: A value below 512 names a row of the context block that the device holds in that stratum; 512 + h names row h of the hub table of the device's index along wide. `counts`: slots at or beyond the count are not live; some device has every slot live in some stratum.
All inputs are finite; a program needn't handle non-finite values.
Results may differ from the reference program's by a relative error of at most 0.0003.
Values sent between devices are 32-bit elements; how exact they have to be, the bound alone decides.
A program may use at most 64 MiB of HBM per device.

```python
import math
import jax
import jax.numpy as jnp
from jax import lax

D = 128
VD = 512
CD = 512
HUB = 2048
EDGES = 1024
BATCH = 512
NNEG = 1024
STRATA = 2
N_NARROW = 16
N_WIDE = 32


def draw_edge_ctx(key, part):
    key = jax.random.fold_in(key, 11)
    key_pick, key_block, key_hub = jax.random.split(key, 3)
    shape = (N_NARROW, N_WIDE, STRATA, EDGES)
    picked = jax.random.randint(key_pick, shape, 0, 2)
    block_row = jax.random.randint(key_block, shape, 0, CD)
    hub_row = jax.random.randint(key_hub, shape, 0, HUB) + CD
    return jnp.where(picked == 1, hub_row, block_row).astype(jnp.int32)


def draw_counts(key, part):
    key = jax.random.fold_in(key, 23)
    key_base, key_spot = jax.random.split(key, 2)
    shape = (N_NARROW, N_WIDE, STRATA)
    base = jax.random.randint(key_base, shape, EDGES // 8, EDGES + 1)
    spot = jax.random.randint(key_spot, (), 0, N_NARROW * N_WIDE * STRATA)
    places = jnp.arange(N_NARROW * N_WIDE * STRATA, dtype=jnp.int32).reshape(shape)
    return jnp.where(places == spot, EDGES, base).astype(jnp.int32)


def with_ends(values, key, smallest, high):
    longest = values.shape.index(max(values.shape))
    spots = []
    for shift in (0, 1):
        where = [jax.random.randint(jax.random.fold_in(key, axis), (), 0, length) for axis, length in enumerate(values.shape)]
        where[longest] = (where[longest] + shift) % values.shape[longest]
        spots.append(tuple(where))
    return values.at[spots[0]].set(smallest).at[spots[1]].set(high)


def shard_levels(rng, shape, cuts, least, top_value):
    def one(axis_at, parts):
        heights = jax.random.uniform(jax.random.fold_in(jax.random.fold_in(rng, 6), axis_at), (parts,), jnp.float32, least / len(cuts), top_value / len(cuts))
        return jnp.repeat(jnp.exp(heights), shape[axis_at] // parts).reshape((-1,) + (1,) * (len(shape) - axis_at - 1))

    gain = one(*cuts[0])
    for cut in cuts[1:]:
        gain = gain * one(*cut)
    return gain


def normal_values(stream_key, extent, deviation, limit, cuts=(), kind=jnp.bfloat16):
    level = shard_levels(stream_key, extent, cuts, -0.22, 0.18) if cuts else 1.0
    array = jax.random.normal(stream_key, extent, jnp.float32) * deviation * level
    return jnp.minimum(jnp.maximum(array, -limit), limit).astype(kind)


def setup_inputs(seed: int = 0) -> dict:
    streams_of = jax.random.split(jax.random.key(seed), 11)
    vertex = normal_values(streams_of[0], (N_NARROW, N_WIDE, VD, D), 0.3, 2.0, ((0, 16), (1, 32)), jnp.float32)
    vertex_state = jnp.clip(jnp.exp(math.log(1.0) - 2.9957323 * jax.random.uniform(streams_of[1], (N_NARROW, N_WIDE, VD), jnp.float32) ** shard_levels(streams_of[1], (N_NARROW, N_WIDE, VD), ((0, 16), (1, 32)), -0.2, 0.2)), 0.05, 1.0)
    context = normal_values(streams_of[2], (N_NARROW, N_WIDE, CD, D), 0.3, 2.0, ((0, 16), (1, 32)), jnp.float32)
    context_state = jnp.clip(jnp.exp(math.log(1.0) - 2.9957323 * jax.random.uniform(streams_of[3], (N_NARROW, N_WIDE, CD), jnp.float32) ** shard_levels(streams_of[3], (N_NARROW, N_WIDE, CD), ((0, 16), (1, 32)), -0.2, 0.2)), 0.05, 1.0)
    hub = normal_values(streams_of[4], (N_WIDE, HUB, D), 0.3, 2.0, ((0, 32),), jnp.float32)
    hub_state = jnp.clip(jnp.exp(math.log(1.0) - 2.9957323 * jax.random.uniform(streams_of[5], (N_WIDE, HUB), jnp.float32) ** shard_levels(streams_of[5], (N_WIDE, HUB), ((0, 32),), -0.2, 0.2)), 0.05, 1.0)
    edge_src = with_ends(jax.random.randint(streams_of[6], (N_NARROW, N_WIDE, STRATA, EDGES), 0, VD), jax.random.fold_in(streams_of[6], 1), 0, VD - 1).astype(jnp.int32)
    edge_ctx = draw_edge_ctx(jax.random.fold_in(streams_of[10], 71), 0)
    negatives = with_ends(jax.random.randint(streams_of[8], (N_NARROW, N_WIDE, STRATA, EDGES // BATCH, NNEG), 0, CD), jax.random.fold_in(streams_of[8], 1), 0, CD - 1).astype(jnp.int32)
    counts = draw_counts(jax.random.fold_in(streams_of[10], 71), 0)
    return dict(vertex=vertex, vertex_state=vertex_state, context=context, context_state=context_state, hub=hub, hub_state=hub_state, edge_src=edge_src, edge_ctx=edge_ctx, negatives=negatives, counts=counts)


LEARN_RATE = 0.5
NEG_WEIGHT = 0.0625

def adagrad(table_rows, row_state, gradient):
    new_state = row_state + lax.optimization_barrier(jnp.mean(gradient * gradient, axis=-1))
    return (table_rows - LEARN_RATE * gradient * lax.rsqrt(new_state)[..., None], new_state)

def stratum(vertex_rows, vertex_sums, block, block_sums, hub_rows, sources, targets, negative_ids, live_count):
    edge_total = sources.shape[0]
    block_len = block.shape[0]
    table = jnp.concatenate([block, hub_rows], axis=0)
    src_vecs = vertex_rows[sources]
    tgt_vecs = table[targets]
    live = (jnp.arange(edge_total) < live_count).astype(vertex_rows.dtype)
    positive = lax.optimization_barrier(jnp.sum(src_vecs * tgt_vecs, axis=1))
    pos_grad = (jax.nn.sigmoid(positive) - 1.0) * live
    batches = negative_ids.shape[0]
    grouped = src_vecs.reshape(batches, -1, src_vecs.shape[1])
    neg_vecs = block[negative_ids]
    scores = jnp.einsum('bik,bjk->bij', grouped, neg_vecs, precision=lax.Precision.HIGHEST)
    neg_grad = NEG_WEIGHT * jax.nn.sigmoid(scores) * live.reshape(batches, -1)[:, :, None]
    pulled = jnp.einsum('bij,bjk->bik', neg_grad, neg_vecs, precision=lax.Precision.HIGHEST)
    src_grad = pos_grad[:, None] * tgt_vecs + pulled.reshape(edge_total, -1)
    neg_rows = jnp.einsum('bij,bik->bjk', neg_grad, grouped, precision=lax.Precision.HIGHEST)
    vertex_grad = jnp.zeros_like(vertex_rows).at[sources].add(src_grad)
    table_grad = jnp.zeros_like(table).at[targets].add(pos_grad[:, None] * src_vecs)
    table_grad = table_grad.at[negative_ids.reshape(-1)].add(neg_rows.reshape(-1, neg_rows.shape[2]))
    new_vertex, new_vsums = adagrad(vertex_rows, vertex_sums, vertex_grad)
    new_block, new_bsums = adagrad(block, block_sums, table_grad[:block_len])
    return (new_vertex, new_vsums, new_block, new_bsums, table_grad[block_len:])

def flatten(values):
    return values.reshape((N_NARROW * N_WIDE,) + values.shape[2:])

def unflatten(values):
    return values.reshape((N_NARROW, N_WIDE) + values.shape[1:])

def run_stratum(stratum_no, vertex_rows, vertex_sums, block, block_sums, hub, edge_src, edge_ctx, negatives, counts):

    def one_device(delta, inputs):
        device_no, vrows, vsums, blk, bsums, srcs, tgts, negs, cnts = inputs
        wide_at = device_no % N_WIDE
        hub_rows = lax.dynamic_index_in_dim(hub, wide_at, 0, keepdims=False)
        result = stratum(vrows, vsums, blk, bsums, hub_rows, srcs[stratum_no], tgts[stratum_no], negs[stratum_no], cnts[stratum_no])
        delta = delta.at[wide_at].add(result[4])
        return (delta, result[:4])
    device_ids = jnp.arange(N_NARROW * N_WIDE, dtype=jnp.int32)
    start = jnp.zeros(hub.shape, hub.dtype)
    delta, outputs = lax.scan(one_device, start, (device_ids, vertex_rows, vertex_sums, block, block_sums, flatten(edge_src), flatten(edge_ctx), flatten(negatives), flatten(counts)))
    return (outputs[0], outputs[1], outputs[2], outputs[3], delta)

def reference(vertex, vertex_state, context, context_state, hub, hub_state, edge_src, edge_ctx, negatives, counts):
    vrows, vsums, block, bsums, delta_first = run_stratum(0, flatten(vertex), flatten(vertex_state), flatten(context), flatten(context_state), hub, edge_src, edge_ctx, negatives, counts)
    block = flatten(jnp.roll(unflatten(block), 1, axis=1))
    bsums = flatten(jnp.roll(unflatten(bsums), 1, axis=1))
    vrows, vsums, block, bsums, delta_second = run_stratum(1, vrows, vsums, block, bsums, hub, edge_src, edge_ctx, negatives, counts)
    hub_mid, state_mid = adagrad(hub, hub_state, delta_first)
    hub_end, state_end = adagrad(hub_mid, state_mid, delta_second)
    return (unflatten(vrows), unflatten(vsums), unflatten(block), unflatten(bsums), hub_end, state_end)
```

```python
import jax
import jax.numpy as jnp
from jax import lax
from jax.experimental import pallas as pl
from jax.experimental.pallas import tpu as pltpu
from jax.sharding import PartitionSpec as P

LEARN_RATE = 0.5
NEG_WEIGHT = 0.0625
MESH = pl.DeviceIdType.MESH
F32 = jnp.float32
BF16 = jnp.bfloat16

D = 128
ROWS = 512
HUB = 2048
EDGES = 1024
BATCH = 512
RING = 4
ORDER = (2, 1, 3, 0)
BLOCK = 128
HALF = 64
PACK = BLOCK + 8


def split(x):
    hi = x.astype(BF16)
    lo = (x - hi.astype(F32)).astype(BF16)
    return hi, lo


def mm(a, b):
    return jnp.dot(a, b, preferred_element_type=F32)


def one_hot(index_row, rows):
    row = lax.broadcasted_iota(jnp.int32, (rows, index_row.shape[1]), 0)
    return jnp.where(row == index_row, 1.0, 0.0).astype(BF16)


def adagrad_block(rows, sums_row, grad):
    old = jnp.broadcast_to(sums_row, (BLOCK, D)).T
    mean = jnp.sum(grad * grad, axis=1, keepdims=True) * (1.0 / D)
    sums = old + mean
    return rows - LEARN_RATE * grad * lax.rsqrt(sums), sums.T[0:1]


def kernel(
    v_ref, vs_ref, c_ref, cs_ref, hub_ref, hs_ref, src_ref, ctx_ref, neg_ref, cnt_ref,
    vo_ref, vso_ref, co_ref, cso_ref, ho_ref, hso_ref,
    hub_t, v_t, c_t, oh_hub, oh_src, oh_blk, chub_t, u_t, u2_t, w2, u2, pos_t, hist, grad_c,
    delta, parts, held, rx, rz, v_mid, block_out, block_in, gathered,
    send_sem, recv_sem, local_sem,
):
    narrow = lax.axis_index("narrow")
    wide = lax.axis_index("wide")
    n_wide = lax.axis_size("wide")
    x = narrow // RING
    z = lax.rem(narrow, RING)

    def at(xx, zz):
        return {"narrow": lax.rem(xx, RING) * RING + lax.rem(zz, RING)}

    x_right, x_left = at(x + 1, z), at(x + 3, z)
    z_right, z_left = at(x, z + 1), at(x, z + 3)
    w_next = {"wide": lax.rem(wide + 1, n_wide)}
    w_prev = {"wide": lax.rem(wide + n_wide - 1, n_wide)}

    barrier = pltpu.get_barrier_semaphore()
    for other in (x_right, x_left, z_right, z_left, w_next, w_prev):
        pl.semaphore_signal(barrier, inc=1, device_id=other, device_id_type=MESH)

    started = []

    def send(src, dst, device):
        slot = len(started)
        copy = pltpu.make_async_remote_copy(
            src_ref=src,
            dst_ref=dst,
            send_sem=send_sem.at[slot],
            recv_sem=recv_sem.at[slot],
            device_id=device,
            device_id_type=MESH,
        )
        copy.start()
        started.append(copy)
        return copy

    def hub_base(zz, xx):
        return pl.multiple_of(
            lax.rem(zz, RING) * (RING * BLOCK) + lax.rem(xx, RING) * BLOCK, BLOCK
        )


    def prepare_hub():
        for part in range(RING):
            rows = pl.ds(part * ROWS, ROWS)
            hi, lo = split(hub_ref[rows, :].T)
            hub_t[0:D, rows] = hi
            hub_t[D : 2 * D, rows] = lo

    def gather_hub(s):
        def body(tile, carry):
            cols = pl.ds(pl.multiple_of(tile * 256, 256), 256)
            hot = one_hot(ctx_ref[s : s + 1, cols] - ROWS, HUB)
            oh_hub[s, :, cols] = hot
            got = mm(hub_t[...], hot)
            chub_t[:, cols] = got[0:D] + got[D : 2 * D]
            return carry

        lax.fori_loop(0, EDGES // 256, body, 0)

    def live_row(s):
        slot = lax.broadcasted_iota(jnp.int32, (1, EDGES), 1)
        return jnp.where(slot < cnt_ref[0, s], 1.0, 0.0)

    def positive(score, live):
        return (0.5 * jnp.tanh(0.5 * score) - 0.5) * live

    def put_rows(ref, value_t):
        for part in range(EDGES // 256):
            hi, lo = split(value_t[:, part * 256 : (part + 1) * 256].T)
            rows = pl.ds(part * 256, 256)
            ref[rows, 0:D] = hi
            ref[rows, D : 2 * D] = lo

    def gather_vertices(s, rows):
        oh_src[...] = one_hot(src_ref[s : s + 1, :], ROWS)
        hi, lo = split(rows.T)
        v_t[0:D, :] = hi
        v_t[D : 2 * D, :] = lo
        got = mm(v_t[...], oh_src[...])
        u2_t[...] = got.astype(BF16)
        u_t[...] = got[0:D] + got[D : 2 * D]

    def hub_gradient(s):
        u = u_t[...]
        score = jnp.sum(u * chub_t[...], axis=0, keepdims=True)
        put_rows(w2, u * positive(score, live_row(s)))

    def hub_piece(s, k):
        rows = pl.ds(hub_base(z + ORDER[k], 0), ROWS)
        got = mm(oh_hub[s, rows, :], w2[...])
        delta[s, rows, :] = got[:, 0:D] + got[:, D : 2 * D]

    def block_edges(s, block):
        live = live_row(s)
        hot = one_hot(ctx_ref[s : s + 1, :], ROWS)
        oh_blk[...] = hot
        hi, lo = split(block.T)
        c_t[0:D, :] = hi
        c_t[D : 2 * D, :] = lo
        got = mm(c_t[...], hot)
        c_all = chub_t[...] + got[0:D] + got[D : 2 * D]
        u = u_t[...]
        score = jnp.sum(u * c_all, axis=0, keepdims=True)
        p = positive(score, live)
        pos_t[...] = p * c_all
        put_rows(w2, u * p)
        put_rows(u2, u * live)
        got = mm(oh_blk[...], w2[...])
        grad_c[...] = got[:, 0:D] + got[:, D : 2 * D]

    def count_negatives(s):
        for b in range(EDGES // BATCH):
            hot = one_hot(neg_ref[s, b : b + 1, :], ROWS)
            hist[s, b] = mm(hot, jnp.ones((hot.shape[1], D), BF16))

    def batch(s, b, block):
        cols = pl.ds(b * BATCH, BATCH)
        hi, lo = split(0.5 * block)
        both = u2_t[:, cols]
        half_score = mm(jnp.concatenate([hi, hi], axis=1), both) + mm(lo, both[0:D])
        q_hi, q_lo = split(0.5 * jnp.tanh(half_score) + 0.5)
        weighted = (NEG_WEIGHT * hist[s, b]) * block
        m_hi, m_lo = split(weighted.T)
        pulled = mm(jnp.concatenate([m_hi, m_lo], axis=0), q_hi)
        pulled = pulled[0:D] + pulled[D : 2 * D] + mm(m_hi, q_lo)
        slot = lax.broadcasted_iota(jnp.int32, (1, BATCH), 1) + b * BATCH
        pos_t[:, cols] += pulled * jnp.where(slot < cnt_ref[0, s], 1.0, 0.0)
        u_rows = u2[cols, :]
        sums = mm(q_hi, u_rows)
        sums = sums[:, 0:D] + sums[:, D : 2 * D] + mm(q_lo, u_rows[:, 0:D])
        grad_c[...] += (NEG_WEIGHT * hist[s, b]) * sums

    def update_vertices(read, write):
        put_rows(w2, pos_t[...])
        got = mm(oh_src[...], w2[...])
        grad = got[:, 0:D] + got[:, D : 2 * D]
        for part in range(ROWS // BLOCK):
            rows = slice(part * BLOCK, (part + 1) * BLOCK)
            write(part, *adagrad_block(*read(part), grad[rows]))

    def update_block(read, write):
        for part in range(ROWS // BLOCK):
            rows = slice(part * BLOCK, (part + 1) * BLOCK)
            write(part, *adagrad_block(*read(part), grad_c[rows, :]))


    x_copies = {}
    z_copies = {}

    def x_first(s, k):
        here = z + ORDER[k]
        two, one, back = hub_base(here, x + 2), hub_base(here, x + 1), hub_base(here, x + 3)
        d = delta.at[s]
        x_copies[s, k] = [
            send(d.at[pl.ds(two, HALF)], rx.at[s, k, 0, 0], x_right),
            send(d.at[pl.ds(two + HALF, HALF)], rx.at[s, k, 1, 0], x_left),
            send(d.at[pl.ds(one + HALF, HALF)], rx.at[s, k, 0, 1], x_right),
            send(d.at[pl.ds(back, HALF)], rx.at[s, k, 1, 1], x_left),
        ]

    def x_second(s, k):
        here = z + ORDER[k]
        one, back = hub_base(here, x + 1), hub_base(here, x + 3)
        d = delta.at[s]
        copies = x_copies[s, k]
        rows = pl.ds(one, HALF)
        copies[0].wait_recv()
        delta[s, rows, :] += rx[s, k, 0, 0]
        copies.append(send(d.at[rows], rx.at[s, k, 0, 2], x_right))
        rows = pl.ds(back + HALF, HALF)
        copies[1].wait_recv()
        delta[s, rows, :] += rx[s, k, 1, 0]
        copies.append(send(d.at[rows], rx.at[s, k, 1, 2], x_left))

    def x_last(s, k):
        mine = hub_base(z + ORDER[k], x)
        copies = x_copies[s, k]
        for copy in copies[2:]:
            copy.wait_recv()
        first = delta[s, pl.ds(mine, HALF), :] + rx[s, k, 0, 2] + rx[s, k, 1, 1]
        second = delta[s, pl.ds(mine + HALF, HALF), :] + rx[s, k, 0, 1] + rx[s, k, 1, 2]
        parts[s, k, 0:HALF, :] = first
        parts[s, k, HALF:BLOCK, :] = second
        part = parts.at[s, k]
        low, high = part.at[pl.ds(0, HALF)], part.at[pl.ds(HALF, HALF)]
        if k == 0:
            z_copies[s] = {
                (0, 0): send(low, rz.at[s, 0, 0], z_right),
                (1, 0): send(high, rz.at[s, 1, 0], z_left),
            }
        elif k == 1:
            z_copies[s][0, 1] = send(high, rz.at[s, 0, 1], z_right)
        elif k == 2:
            z_copies[s][1, 1] = send(low, rz.at[s, 1, 1], z_left)

    def z_second(s):
        copies = z_copies[s]
        copies[0, 0].wait_recv()
        parts[s, 1, 0:HALF, :] += rz[s, 0, 0]
        copies[0, 2] = send(parts.at[s, 1].at[pl.ds(0, HALF)], rz.at[s, 0, 2], z_right)
        copies[1, 0].wait_recv()
        parts[s, 2, HALF:BLOCK, :] += rz[s, 1, 0]
        copies[1, 2] = send(parts.at[s, 2].at[pl.ds(HALF, HALF)], rz.at[s, 1, 2], z_left)

    def z_last(s):
        copies = z_copies[s]
        for key in ((0, 1), (1, 1), (0, 2), (1, 2)):
            copies[key].wait_recv()
        first = parts[s, 3, 0:HALF, :] + rz[s, 0, 2] + rz[s, 1, 1]
        second = parts[s, 3, HALF:BLOCK, :] + rz[s, 0, 1] + rz[s, 1, 2]
        return jnp.concatenate([first, second], axis=0)


    prepare_hub()
    gather_hub(0)
    gather_vertices(0, v_ref[...])
    hub_gradient(0)
    pl.semaphore_wait(barrier, 6)
    for k in range(RING):
        hub_piece(0, k)
        x_first(0, k)
    block_edges(0, c_ref[...])
    count_negatives(0)
    for b in range(EDGES // BATCH):
        batch(0, b, c_ref[...])
    for k in range(RING):
        x_second(0, k)

    def part_of(part):
        return pl.ds(part * BLOCK, BLOCK)

    def read_vertex(part):
        return v_ref[part_of(part), :], vs_ref[:, part_of(part)]

    def write_vertex_mid(part, rows, sums):
        v_mid[part_of(part), :] = rows
        vso_ref[:, part_of(part)] = sums

    def read_block(part):
        return c_ref[part_of(part), :], cs_ref[:, part_of(part)]

    def write_block_out(part, rows, sums):
        block_out[part_of(part), :] = rows
        block_out[ROWS + part : ROWS + part + 1, :] = sums

    update_block(read_block, write_block_out)
    for part in range(ROWS // BLOCK, 8):
        block_out[ROWS + part : ROWS + part + 1, :] = jnp.zeros((1, D), F32)
    shift = send(block_out, block_in, w_next)
    update_vertices(read_vertex, write_vertex_mid)


    gather_hub(1)
    gather_vertices(1, v_mid[...])
    hub_gradient(1)
    for k in range(RING):
        hub_piece(1, k)
        x_first(1, k)
        x_last(0, k)
    count_negatives(1)
    z_second(0)
    shift.wait_recv()
    block_edges(1, block_in[0:ROWS, :])
    for k in range(RING):
        x_second(1, k)
    own = hub_base(z, x)
    own_rows = hub_ref[pl.ds(own, BLOCK), :]
    mid_rows, mid_sums = adagrad_block(own_rows, hs_ref[:, pl.ds(own, BLOCK)], z_last(0))
    held[0:BLOCK, :] = mid_rows
    held[BLOCK : BLOCK + 1, :] = mid_sums
    for b in range(EDGES // BATCH):
        batch(1, b, block_in[0:ROWS, :])
        x_last(1, 2 * b)
        x_last(1, 2 * b + 1)
    z_second(1)

    def read_vertex_mid(part):
        return v_mid[part_of(part), :], vso_ref[:, part_of(part)]

    def write_vertex(part, rows, sums):
        vo_ref[part_of(part), :] = rows
        vso_ref[:, part_of(part)] = sums

    def read_block_in(part):
        return block_in[part_of(part), :], block_in[ROWS + part : ROWS + part + 1, :]

    def write_block(part, rows, sums):
        co_ref[part_of(part), :] = rows
        cso_ref[:, part_of(part)] = sums


    end_rows, end_sums = adagrad_block(
        held[0:BLOCK, :], held[BLOCK : BLOCK + 1, :], z_last(1)
    )

    def slot_of(zz, xx):
        return lax.rem(zz, RING) * RING + lax.rem(xx, RING)

    me = slot_of(z, x)
    gathered[me, 0:BLOCK, :] = end_rows
    gathered[me, BLOCK:PACK, :] = jnp.broadcast_to(end_sums, (8, D))

    def spread(slot, device, lo=0, n=PACK):
        block = gathered.at[slot].at[pl.ds(lo, n)]
        return send(block, block, device)

    stores = []

    def store(zz, xx):
        slot = slot_of(zz, xx)
        copy = pltpu.make_async_copy(
            gathered.at[slot].at[pl.ds(0, BLOCK)],
            ho_ref.at[pl.ds(hub_base(zz, xx), BLOCK)],
            local_sem.at[len(stores)],
        )
        copy.start()
        stores.append(copy)
        hso_ref[:, pl.ds(hub_base(zz, xx), BLOCK)] = gathered[slot, BLOCK : BLOCK + 1, :]

    z_r = spread(me, z_right)
    z_l = spread(me, z_left)
    direct = {0: (spread(me, x_right), spread(me, x_left))}
    store(z, x)
    update_vertices(read_vertex_mid, write_vertex)
    update_block(read_block_in, write_block)

    z_r.wait_recv()
    from_left = slot_of(z + 3, x)
    z_fr = spread(from_left, z_right, 0, HALF)
    direct[3] = (spread(from_left, x_right), spread(from_left, x_left))
    store(z + 3, x)
    z_l.wait_recv()
    from_right = slot_of(z + 1, x)
    z_fl = spread(from_right, z_left, HALF, PACK - HALF)
    direct[1] = (spread(from_right, x_right), spread(from_right, x_left))
    store(z + 1, x)

    forwards = {}

    def forward(dz):
        right, left = direct[dz]
        right.wait_recv()
        fr = spread(slot_of(z + dz, x + 3), x_right, 0, HALF)
        store(z + dz, x + 3)
        left.wait_recv()
        fl = spread(slot_of(z + dz, x + 1), x_left, HALF, PACK - HALF)
        store(z + dz, x + 1)
        forwards[dz] = (fr, fl)

    def finish(dz):
        fr, fl = forwards[dz]
        fr.wait_recv()
        fl.wait_recv()
        store(z + dz, x + 2)

    forward(0)
    z_fr.wait_recv()
    z_fl.wait_recv()
    far = slot_of(z + 2, x)
    direct[2] = (spread(far, x_right), spread(far, x_left))
    store(z + 2, x)
    for dz in (3, 1, 2):
        forward(dz)
    for dz in (0, 3, 1, 2):
        finish(dz)

    for copy in started:
        copy.wait_send()
    for copy in stores:
        copy.wait()


N_COPIES = 2 * 24 + 2 * 6 + 1 + 4 + 16


def per_device(
    vertex, vertex_state, context, context_state, hub, hub_state, edge_src, edge_ctx, negatives, counts
):
    vmem = pl.BlockSpec(memory_space=pltpu.VMEM)
    shapes = (
        jax.ShapeDtypeStruct((ROWS, D), F32),
        jax.ShapeDtypeStruct((1, ROWS), F32),
        jax.ShapeDtypeStruct((ROWS, D), F32),
        jax.ShapeDtypeStruct((1, ROWS), F32),
        jax.ShapeDtypeStruct((HUB, D), F32),
        jax.ShapeDtypeStruct((1, HUB), F32),
    )
    scratch = [
        pltpu.VMEM((2 * D, HUB), BF16),
        pltpu.VMEM((2 * D, ROWS), BF16),
        pltpu.VMEM((2 * D, ROWS), BF16),
        pltpu.VMEM((2, HUB, EDGES), BF16),
        pltpu.VMEM((ROWS, EDGES), BF16),
        pltpu.VMEM((ROWS, EDGES), BF16),
        pltpu.VMEM((D, EDGES), F32),
        pltpu.VMEM((D, EDGES), F32),
        pltpu.VMEM((2 * D, EDGES), BF16),
        pltpu.VMEM((EDGES, 2 * D), BF16),
        pltpu.VMEM((EDGES, 2 * D), BF16),
        pltpu.VMEM((D, EDGES), F32),
        pltpu.VMEM((2, 2, ROWS, D), F32),
        pltpu.VMEM((ROWS, D), F32),
        pltpu.VMEM((2, HUB, D), F32),
        pltpu.VMEM((2, RING, BLOCK, D), F32),
        pltpu.VMEM((PACK, D), F32),
        pltpu.VMEM((2, RING, 2, 3, HALF, D), F32),
        pltpu.VMEM((2, 2, 3, HALF, D), F32),
        pltpu.VMEM((ROWS, D), F32),
        pltpu.VMEM((ROWS + 8, D), F32),
        pltpu.VMEM((ROWS + 8, D), F32),
        pltpu.VMEM((RING * RING, PACK, D), F32),
        pltpu.SemaphoreType.DMA((N_COPIES,)),
        pltpu.SemaphoreType.DMA((N_COPIES,)),
        pltpu.SemaphoreType.DMA((RING * RING,)),
    ]
    out = pl.pallas_call(
        kernel,
        out_shape=shapes,
        in_specs=[vmem] * 9 + [pl.BlockSpec(memory_space=pltpu.SMEM)],
        out_specs=(vmem, vmem, vmem, vmem, pl.BlockSpec(memory_space=pl.ANY), vmem),
        scratch_shapes=scratch,
        compiler_params=pltpu.CompilerParams(
            collective_id=0, has_side_effects=True, vmem_limit_bytes=56 * 1024 * 1024
        ),
        name="skipgram_window",
    )(
        vertex[0, 0],
        vertex_state[0],
        context[0, 0],
        context_state[0],
        hub[0],
        hub_state,
        edge_src[0, 0],
        edge_ctx[0, 0],
        negatives[0, 0],
        counts[0],
    )
    return (
        out[0][None, None],
        out[1][None],
        out[2][None, None],
        out[3][None],
        out[4][None],
        out[5],
    )


def solution(mesh):
    narrow_wide = lambda n: P("narrow", "wide", *([None] * n))
    in_specs = (
        narrow_wide(2),
        narrow_wide(1),
        narrow_wide(2),
        narrow_wide(1),
        P("wide", None, None),
        P("wide", None),
        narrow_wide(2),
        narrow_wide(2),
        narrow_wide(3),
        narrow_wide(1),
    )
    out_specs = (
        narrow_wide(2),
        narrow_wide(1),
        narrow_wide(2),
        narrow_wide(1),
        P("wide", None, None),
        P("wide", None),
    )
    return jax.shard_map(
        per_device, mesh=mesh, in_specs=in_specs, out_specs=out_specs, check_vma=False
    )
```

```python
import jax
import jax.numpy as jnp
from jax import lax
from jax.experimental import pallas as pl
from jax.experimental.pallas import tpu as pltpu
from jax.sharding import PartitionSpec as P

LEARN_RATE = 0.5
NEG_WEIGHT = 0.0625
MESH = pl.DeviceIdType.MESH
F32 = jnp.float32
BF16 = jnp.bfloat16

D = 128
ROWS = 512
HUB = 2048
EDGES = 1024
BATCH = 512
RING = 4
ORDER = (2, 1, 3, 0)
BLOCK = 128
HALF = 64
FIRST = ((0, 0, 128, "x"),)
SECOND = (((1, 0, 64, "x"),), ((1, 64, 64, "x"),))
DIRECT = SECOND[0] + SECOND[1]
PACK = HALF + 8


def split(x):
    hi = x.astype(BF16)
    lo = (x - hi.astype(F32)).astype(BF16)
    return hi, lo


def mm(a, b):
    return jnp.dot(a, b, preferred_element_type=F32)


def one_hot(index_row, rows):
    row = lax.broadcasted_iota(jnp.int32, (rows, index_row.shape[1]), 0)
    return jnp.where(row == index_row, 1.0, 0.0).astype(BF16)


def adagrad_block(rows, sums_row, grad):
    old = jnp.broadcast_to(sums_row, (BLOCK, D)).T
    mean = jnp.sum(grad * grad, axis=1, keepdims=True) * (1.0 / D)
    sums = old + mean
    return rows - LEARN_RATE * grad * lax.rsqrt(sums), sums.T[0:1]


def kernel(
    v_ref, vs_ref, c_ref, cs_ref, hub_ref, hs_ref, src_ref, ctx_ref, neg_ref, cnt_ref,
    vo_ref, vso_ref, co_ref, cso_ref, gathered,
    hub_t, v_t, c_t, oh_hub, oh_src, oh_blk, chub_t, u_t, u2_t, w2, u2, pos_t, pu_t, live_u_t,
    q_parts, hist, grad_c, delta, parts, mid_rows, mid_sums, far, rx, rz, v_mid, block_out, block_in,
    send_sem, recv_sem,
):
    narrow = lax.axis_index("narrow")
    wide = lax.axis_index("wide")
    n_wide = lax.axis_size("wide")
    x = narrow // RING
    z = lax.rem(narrow, RING)

    def at(xx, zz):
        return {"narrow": lax.rem(xx, RING) * RING + lax.rem(zz, RING)}

    x_right, x_left = at(x + 1, z), at(x + 3, z)
    z_right, z_left = at(x, z + 1), at(x, z + 3)
    x_far, z_far = at(x + 2, z), at(x, z + 2)
    w_next = {"wide": lax.rem(wide + 1, n_wide)}
    w_prev = {"wide": lax.rem(wide + n_wide - 1, n_wide)}

    barrier = pltpu.get_barrier_semaphore()
    for other in (x_right, x_left, x_far, z_right, z_left, z_far, w_next, w_prev):
        pl.semaphore_signal(barrier, inc=1, device_id=other, device_id_type=MESH)

    started = []

    def send(src, dst, device):
        slot = len(started)
        copy = pltpu.make_async_remote_copy(
            src_ref=src,
            dst_ref=dst,
            send_sem=send_sem.at[slot],
            recv_sem=recv_sem.at[slot],
            device_id=device,
            device_id_type=MESH,
        )
        copy.start()
        started.append(copy)
        return copy

    def hub_base(zz, xx):
        return pl.multiple_of(
            lax.rem(zz, RING) * (RING * BLOCK) + lax.rem(xx, RING) * BLOCK, BLOCK
        )


    def prepare_hub():
        for part in range(RING):
            rows = pl.ds(part * ROWS, ROWS)
            hi, lo = split(hub_ref[rows, :].T)
            hub_t[0:D, rows] = hi
            hub_t[D : 2 * D, rows] = lo

    def gather_hub(s):
        def body(tile, carry):
            cols = pl.ds(pl.multiple_of(tile * 256, 256), 256)
            hot = one_hot(ctx_ref[s : s + 1, cols] - ROWS, HUB)
            oh_hub[s, :, cols] = hot
            got = mm(hub_t[...], hot)
            chub_t[:, cols] = got[0:D] + got[D : 2 * D]
            return carry

        lax.fori_loop(0, EDGES // 256, body, 0)

    def live_row(s):
        slot = lax.broadcasted_iota(jnp.int32, (1, EDGES), 1)
        return jnp.where(slot < cnt_ref[0, s], 1.0, 0.0)

    def positive(score, live):
        return (0.5 * jnp.tanh(0.5 * score) - 0.5) * live

    def put_rows(ref, value_t):
        for part in range(EDGES // 256):
            hi, lo = split(value_t[:, part * 256 : (part + 1) * 256].T)
            rows = pl.ds(part * 256, 256)
            ref[rows, 0:D] = hi
            ref[rows, D : 2 * D] = lo

    def gather_vertices(s, rows):
        oh_src[...] = one_hot(src_ref[s : s + 1, :], ROWS)
        hi, lo = split(rows.T)
        v_t[0:D, :] = hi
        v_t[D : 2 * D, :] = lo
        got = mm(v_t[...], oh_src[...])
        u2_t[...] = got.astype(BF16)
        u_t[...] = got[0:D] + got[D : 2 * D]

    def hub_gradient(s):
        u = u_t[...]
        score = jnp.sum(u * chub_t[...], axis=0, keepdims=True)
        put_rows(w2, u * positive(score, live_row(s)))

    def hub_piece(s, k):
        rows = pl.ds(hub_base(z + ORDER[k], 0), ROWS)
        got = mm(oh_hub[s, rows, :], w2[...])
        delta[s, rows, :] = got[:, 0:D] + got[:, D : 2 * D]

    def block_edges(s, block):
        live = live_row(s)
        oh_blk[...] = one_hot(ctx_ref[s : s + 1, :], ROWS)
        hi, lo = split(block.T)
        c_t[0:D, :] = hi
        c_t[D : 2 * D, :] = lo
        got = mm(c_t[...], oh_blk[...])
        c_all = chub_t[...] + got[0:D] + got[D : 2 * D]
        u = u_t[...]
        score = jnp.sum(u * c_all, axis=0, keepdims=True)
        p = positive(score, live)
        pos_t[...] = p * c_all
        pu_t[...] = u * p
        live_u_t[...] = u * live

    def count_negatives(s):
        for b in range(EDGES // BATCH):
            hot = one_hot(neg_ref[s, b : b + 1, :], ROWS)
            hist[s, b] = mm(hot, jnp.ones((hot.shape[1], D), BF16))

    def batch(s, b, block):
        cols = pl.ds(b * BATCH, BATCH)
        hi, lo = split(0.5 * block)
        both = u2_t[:, cols]
        half_score = mm(jnp.concatenate([hi, hi], axis=1), both) + mm(lo, both[0:D])
        q_hi, q_lo = split(0.5 * jnp.tanh(half_score) + 0.5)
        q_parts[0, :, cols] = q_hi
        q_parts[1, :, cols] = q_lo
        weighted = (NEG_WEIGHT * hist[s, b]) * block
        m_hi, m_lo = split(weighted.T)
        pulled = mm(jnp.concatenate([m_hi, m_lo], axis=0), q_hi)
        pulled = pulled[0:D] + pulled[D : 2 * D] + mm(m_hi, q_lo)
        slot = lax.broadcasted_iota(jnp.int32, (1, BATCH), 1) + b * BATCH
        pos_t[:, cols] += pulled * jnp.where(slot < cnt_ref[0, s], 1.0, 0.0)

    def block_gradient(s):
        put_rows(u2, pu_t[...])
        got = mm(oh_blk[...], u2[...])
        total = got[:, 0:D] + got[:, D : 2 * D]
        put_rows(u2, live_u_t[...])
        for b in range(EDGES // BATCH):
            cols = pl.ds(b * BATCH, BATCH)
            u_rows = u2[cols, :]
            got = mm(q_parts[0, :, cols], u_rows)
            got = got[:, 0:D] + got[:, D : 2 * D] + mm(q_parts[1, :, cols], u_rows[:, 0:D])
            total = total + (NEG_WEIGHT * hist[s, b]) * got
        grad_c[...] = total

    def update_vertices(read, write):
        put_rows(w2, pos_t[...])
        got = mm(oh_src[...], w2[...])
        grad = got[:, 0:D] + got[:, D : 2 * D]
        for part in range(ROWS // BLOCK):
            rows = slice(part * BLOCK, (part + 1) * BLOCK)
            write(part, *adagrad_block(*read(part), grad[rows]))

    def update_block(read, write):
        for part in range(ROWS // BLOCK):
            rows = slice(part * BLOCK, (part + 1) * BLOCK)
            write(part, *adagrad_block(*read(part), grad_c[rows, :]))


    ring_copies = {}
    cross_copies = {}

    def base_of(part, along, across):
        if part[3] == "x":
            return hub_base(z + across, x + along) + part[1]
        return hub_base(z + along, x + across) + part[1]

    def device_of(part, along, across):
        return at(x + along, z + across) if part[3] == "x" else at(x + across, z + along)

    def ring_first(part, k):
        s, lo, n, _ = part
        half = n // 2
        right, left = device_of(part, 1, 0), device_of(part, 3, 0)
        two, one, back = (base_of(part, d, ORDER[k]) for d in (2, 1, 3))
        d = delta.at[s]

        def land(way, kind):
            return rx.at[s, k, way, kind].at[pl.ds(lo // 2, half)]

        if k == 0 and part in DIRECT:
            ring_copies[part, k] = [
                send(d.at[pl.ds(two, n)], far.at[s, 0].at[pl.ds(lo, n)], device_of(part, 2, 0)),
                send(d.at[pl.ds(one, n)], far.at[s, 1].at[pl.ds(lo, n)], right),
                send(d.at[pl.ds(back, n)], far.at[s, 2].at[pl.ds(lo, n)], left),
            ]
            return
        ring_copies[part, k] = [
            send(d.at[pl.ds(two, half)], land(0, 0), right),
            send(d.at[pl.ds(two + half, half)], land(1, 0), left),
            send(d.at[pl.ds(one + half, half)], land(0, 1), right),
            send(d.at[pl.ds(back, half)], land(1, 1), left),
        ]

    def ring_second(part, k):
        if k == 0 and part in DIRECT:
            return
        s, lo, n, _ = part
        half = n // 2
        one, back = (base_of(part, d, ORDER[k]) for d in (1, 3))
        d = delta.at[s]
        got = pl.ds(lo // 2, half)
        copies = ring_copies[part, k]
        rows = pl.ds(one, half)
        copies[0].wait_recv()
        delta[s, rows, :] += rx[s, k, 0, 0, got, :]
        copies.append(send(d.at[rows], rx.at[s, k, 0, 2].at[got], device_of(part, 1, 0)))
        rows = pl.ds(back + half, half)
        copies[1].wait_recv()
        delta[s, rows, :] += rx[s, k, 1, 0, got, :]
        copies.append(send(d.at[rows], rx.at[s, k, 1, 2].at[got], device_of(part, 3, 0)))

    def ring_last(part, k):
        s, lo, n, _ = part
        half = n // 2
        mine = base_of(part, 0, ORDER[k])
        copies = ring_copies[part, k]
        whole = pl.ds(lo, n)
        if k == 0 and part in DIRECT:
            total = delta[s, pl.ds(mine, n), :]
            for way in (1, 2, 0):
                copies[way].wait_recv()
                total = total + far[s, way, whole, :]
            parts[s, k, whole, :] = total
        else:
            got = pl.ds(lo // 2, half)
            for copy in copies[2:]:
                copy.wait_recv()
            parts[s, k, pl.ds(lo, half), :] = (
                delta[s, pl.ds(mine, half), :] + rx[s, k, 0, 2, got, :] + rx[s, k, 1, 1, got, :]
            )
            parts[s, k, pl.ds(lo + half, half), :] = (
                delta[s, pl.ds(mine + half, half), :]
                + rx[s, k, 0, 1, got, :]
                + rx[s, k, 1, 2, got, :]
            )
        if ORDER[k]:
            cross_copies[part, k] = send(
                parts.at[s, k].at[whole], rz.at[s, k].at[whole], device_of(part, 0, ORDER[k])
            )

    def reduced(part):
        s, lo, n, _ = part
        whole = pl.ds(lo, n)
        total = parts[s, RING - 1, whole, :]
        for k in (1, 2, 0):
            cross_copies[part, k].wait_recv()
            total = total + rz[s, k, whole, :]
        return total

    def each(function, parts_, pieces=(0, 1, 2, 3)):
        for part in parts_:
            for k in pieces:
                function(part, k)


    def slot_of(zz, xx):
        return lax.rem(zz, RING) * RING + lax.rem(xx, RING)

    me = slot_of(z, x)
    gathers = {}

    def spread(h, slot, device, lo=0, n=PACK):
        block = gathered.at[slot, h].at[pl.ds(lo, n)]
        return send(block, block, device)

    def gather_first(h):
        rows = pl.ds(h * HALF, HALF)
        grad = jnp.concatenate([reduced(part) for part in SECOND[h]], axis=0)
        sums = mid_sums[rows, :] + jnp.sum(grad * grad, axis=1, keepdims=True) * (1.0 / D)
        gathered[me, h, 0:HALF, :] = mid_rows[rows, :] - LEARN_RATE * grad * lax.rsqrt(sums)
        none = jnp.zeros((HALF, D), F32)
        column = jnp.concatenate([sums, none] if h == 0 else [none, sums], axis=0)
        gathered[me, h, HALF:PACK, :] = column.T[0:8]
        z_l, z_r = spread(h, me, z_left), spread(h, me, z_right)
        z_two = spread(h, me, z_far)
        gathers[h] = {
            "z": (z_r, z_l, z_two),
            0: (spread(h, me, x_right), spread(h, me, x_left)),
            "last": [],
        }

    def gather_near(h):
        z_r, z_l, _ = gathers[h]["z"]
        for copy, dz in ((z_r, 3), (z_l, 1)):
            copy.wait_recv()
            slot = slot_of(z + dz, x)
            gathers[h][dz] = (spread(h, slot, x_right), spread(h, slot, x_left))

    def gather_far(h):
        gathers[h]["z"][2].wait_recv()
        slot = slot_of(z + 2, x)
        for device in (x_far, x_right, x_left):
            gathers[h]["last"].append(spread(h, slot, device))

    def forward(h, dz):
        right, left = gathers[h][dz]
        last = gathers[h]["last"]
        right.wait_recv()
        last.append(spread(h, slot_of(z + dz, x + 3), x_right, 0, HALF // 2))
        left.wait_recv()
        last.append(spread(h, slot_of(z + dz, x + 1), x_left, HALF // 2, PACK - HALF // 2))


    def part_of(part):
        return pl.ds(part * BLOCK, BLOCK)

    def read_vertex(part):
        return v_ref[part_of(part), :], vs_ref[:, part_of(part)]

    def write_vertex_mid(part, rows, sums):
        v_mid[part_of(part), :] = rows
        vso_ref[:, part_of(part)] = sums

    def read_block(part):
        return c_ref[part_of(part), :], cs_ref[:, part_of(part)]

    def write_block_out(part, rows, sums):
        block_out[part_of(part), :] = rows
        block_out[ROWS + part : ROWS + part + 1, :] = sums

    def read_vertex_mid(part):
        return v_mid[part_of(part), :], vso_ref[:, part_of(part)]

    def write_vertex(part, rows, sums):
        vo_ref[part_of(part), :] = rows
        vso_ref[:, part_of(part)] = sums

    def read_block_in(part):
        return block_in[part_of(part), :], block_in[ROWS + part : ROWS + part + 1, :]

    def write_block(part, rows, sums):
        co_ref[part_of(part), :] = rows
        cso_ref[:, part_of(part)] = sums

    prepare_hub()
    gather_hub(0)
    gather_vertices(0, v_ref[...])
    hub_gradient(0)
    pl.semaphore_wait(barrier, 8)
    for k in range(RING):
        hub_piece(0, k)
        each(ring_first, [p for p in FIRST if p[3] == "x"], [k])
    each(ring_first, [p for p in FIRST if p[3] == "z"])
    block_edges(0, c_ref[...])
    count_negatives(0)
    batch(0, 0, c_ref[...])
    each(ring_second, FIRST)
    batch(0, 1, c_ref[...])
    each(ring_last, FIRST, [0])
    update_vertices(read_vertex, write_vertex_mid)


    gather_hub(1)
    each(ring_last, FIRST, [1, 2, 3])
    gather_vertices(1, v_mid[...])
    hub_gradient(1)
    for k in range(RING):
        hub_piece(1, k)
        each(ring_first, [p for p in SECOND[0] if p[3] == "x"], [k])
    each(ring_first, [p for p in SECOND[0] if p[3] == "z"])
    each(ring_first, SECOND[1])

    block_gradient(0)
    update_block(read_block, write_block_out)
    for part in range(ROWS // BLOCK, 8):
        block_out[ROWS + part : ROWS + part + 1, :] = jnp.zeros((1, D), F32)
    shift = send(block_out, block_in, w_next)
    count_negatives(1)
    each(ring_second, SECOND[0])
    each(ring_last, SECOND[0], [0])
    each(ring_second, SECOND[1])
    each(ring_last, SECOND[1], [0])
    own = pl.ds(hub_base(z, x), BLOCK)
    old = jnp.broadcast_to(hs_ref[:, own], (BLOCK, D)).T
    grad = jnp.concatenate([reduced(part) for part in FIRST], axis=0)
    sums = old + jnp.sum(grad * grad, axis=1, keepdims=True) * (1.0 / D)
    mid_sums[...] = sums
    mid_rows[...] = hub_ref[own, :] - LEARN_RATE * grad * lax.rsqrt(sums)
    shift.wait_recv()
    block_edges(1, block_in[0:ROWS, :])
    each(ring_last, SECOND[0], [1, 2, 3])
    batch(1, 0, block_in[0:ROWS, :])
    each(ring_last, SECOND[1], [1, 2, 3])
    batch(1, 1, block_in[0:ROWS, :])
    gather_first(0)
    update_vertices(read_vertex_mid, write_vertex)
    gather_first(1)
    block_gradient(1)
    update_block(read_block_in, write_block)
    gather_near(0)
    forward(0, 0)
    gather_far(0)
    gather_near(1)
    forward(0, 3)
    forward(0, 1)
    forward(1, 0)
    gather_far(1)
    forward(1, 3)
    forward(1, 1)
    for h in range(2):
        for copy in gathers[h]["last"]:
            copy.wait_recv()
    for copy in started:
        copy.wait_send()


def place(vo, vso, co, cso, rows, vo_ref, vso_ref, co_ref, cso_ref, ho_ref, hso_ref, sem):
    copies = [
        pltpu.make_async_copy(rows.at[:, :, pl.ds(0, HALF), :], ho_ref, sem.at[0]),
        pltpu.make_async_copy(vo, vo_ref, sem.at[1]),
        pltpu.make_async_copy(co, co_ref, sem.at[2]),
    ]
    for copy in copies:
        copy.start()
    vso_ref[...] = vso[...]
    cso_ref[...] = cso[...]
    for block in range(RING * RING):
        hso_ref[:, block * BLOCK : (block + 1) * BLOCK] = (
            rows[block, 0, HALF : HALF + 1, :] + rows[block, 1, HALF : HALF + 1, :]
        )
    for copy in copies:
        copy.wait()


PARTS = FIRST + SECOND[0] + SECOND[1]
N_COPIES = sum(27 - 3 * (p in DIRECT) for p in PARTS) + 1 + 2 * (3 + 3 * 4 + 3)


def per_device(
    vertex, vertex_state, context, context_state, hub, hub_state, edge_src, edge_ctx, negatives, counts
):
    vmem = pl.BlockSpec(memory_space=pltpu.VMEM)
    inner = (
        pltpu.VMEM((ROWS, D), F32),
        pltpu.VMEM((1, ROWS), F32),
        pltpu.VMEM((ROWS, D), F32),
        pltpu.VMEM((1, ROWS), F32),
        pltpu.VMEM((RING * RING, 2, PACK, D), F32),
    )
    shapes = (
        jax.ShapeDtypeStruct((ROWS, D), F32),
        jax.ShapeDtypeStruct((1, ROWS), F32),
        jax.ShapeDtypeStruct((ROWS, D), F32),
        jax.ShapeDtypeStruct((1, ROWS), F32),
        jax.ShapeDtypeStruct((RING * RING, 2, HALF, D), F32),
        jax.ShapeDtypeStruct((1, HUB), F32),
    )
    scratch = [
        pltpu.VMEM((2 * D, HUB), BF16),
        pltpu.VMEM((2 * D, ROWS), BF16),
        pltpu.VMEM((2 * D, ROWS), BF16),
        pltpu.VMEM((2, HUB, EDGES), BF16),
        pltpu.VMEM((ROWS, EDGES), BF16),
        pltpu.VMEM((ROWS, EDGES), BF16),
        pltpu.VMEM((D, EDGES), F32),
        pltpu.VMEM((D, EDGES), F32),
        pltpu.VMEM((2 * D, EDGES), BF16),
        pltpu.VMEM((EDGES, 2 * D), BF16),
        pltpu.VMEM((EDGES, 2 * D), BF16),
        pltpu.VMEM((D, EDGES), F32),
        pltpu.VMEM((D, EDGES), F32),
        pltpu.VMEM((D, EDGES), F32),
        pltpu.VMEM((2, ROWS, EDGES), BF16),
        pltpu.VMEM((2, 2, ROWS, D), F32),
        pltpu.VMEM((ROWS, D), F32),
        pltpu.VMEM((2, HUB, D), F32),
        pltpu.VMEM((2, RING, BLOCK, D), F32),
        pltpu.VMEM((BLOCK, D), F32),
        pltpu.VMEM((BLOCK, D), F32),
        pltpu.VMEM((2, 3, BLOCK, D), F32),
        pltpu.VMEM((2, RING, 2, 3, HALF, D), F32),
        pltpu.VMEM((2, RING - 1, BLOCK, D), F32),
        pltpu.VMEM((ROWS, D), F32),
        pltpu.VMEM((ROWS + 8, D), F32),
        pltpu.VMEM((ROWS + 8, D), F32),
        pltpu.SemaphoreType.DMA((N_COPIES,)),
        pltpu.SemaphoreType.DMA((N_COPIES,)),
    ]
    found = pl.pallas_call(
        kernel,
        out_shape=inner,
        in_specs=[vmem] * 9 + [pl.BlockSpec(memory_space=pltpu.SMEM)],
        out_specs=[vmem] * 5,
        scratch_shapes=scratch,
        compiler_params=pltpu.CompilerParams(
            collective_id=0, has_side_effects=True, vmem_limit_bytes=58 * 1024 * 1024
        ),
        name="skipgram_window",
    )(
        vertex[0, 0],
        vertex_state[0],
        context[0, 0],
        context_state[0],
        hub[0],
        hub_state,
        edge_src[0, 0],
        edge_ctx[0, 0],
        negatives[0, 0],
        counts[0],
    )
    hbm = pl.BlockSpec(memory_space=pl.ANY)
    out = pl.pallas_call(
        place,
        out_shape=shapes,
        in_specs=[vmem] * 5,
        out_specs=(hbm, vmem, hbm, vmem, hbm, vmem),
        scratch_shapes=[pltpu.SemaphoreType.DMA((3,))],
        compiler_params=pltpu.CompilerParams(vmem_limit_bytes=4 * 1024 * 1024),
        name="place_results",
    )(*found)
    return (
        out[0][None, None],
        out[1][None],
        out[2][None, None],
        out[3][None],
        out[4].reshape(1, HUB, D),
        out[5],
    )


def solution(mesh):
    narrow_wide = lambda n: P("narrow", "wide", *([None] * n))
    in_specs = (
        narrow_wide(2),
        narrow_wide(1),
        narrow_wide(2),
        narrow_wide(1),
        P("wide", None, None),
        P("wide", None),
        narrow_wide(2),
        narrow_wide(2),
        narrow_wide(3),
        narrow_wide(1),
    )
    out_specs = (
        narrow_wide(2),
        narrow_wide(1),
        narrow_wide(2),
        narrow_wide(1),
        P("wide", None, None),
        P("wide", None),
    )
    return jax.shard_map(
        per_device, mesh=mesh, in_specs=in_specs, out_specs=out_specs, check_vma=False
    )
```

```python
import jax
import jax.numpy as jnp
from jax import lax
from jax.experimental import pallas as pl
from jax.experimental.pallas import tpu as pltpu
from jax.sharding import PartitionSpec as P

LEARN_RATE = 0.5
NEG_WEIGHT = 0.0625
MESH = pl.DeviceIdType.MESH
F32 = jnp.float32
BF16 = jnp.bfloat16

D = 128
ROWS = 512
HUB = 2048
EDGES = 1024
BATCH = 512
RING = 4
ORDER = (2, 1, 3, 0)
BLOCK = 128
HALF = 64
FIRST = ((0, 0, 128, "x"),)
SECOND = (((1, 0, 64, "x"),), ((1, 64, 64, "x"),))
DIRECT = SECOND[0] + SECOND[1]
PACK = HALF + 8


def split(x):
    hi = x.astype(BF16)
    lo = (x - hi.astype(F32)).astype(BF16)
    return hi, lo


def mm(a, b):
    return jnp.dot(a, b, preferred_element_type=F32)


def one_hot(index_row, rows):
    row = lax.broadcasted_iota(jnp.int16, (rows, index_row.shape[1]), 0)
    one, none = jnp.ones((), BF16), jnp.zeros((), BF16)
    return jnp.where(row == index_row.astype(jnp.int16), one, none)


def adagrad_block(rows, sums_row, grad):
    old = jnp.broadcast_to(sums_row, (BLOCK, D)).T
    mean = jnp.sum(grad * grad, axis=1, keepdims=True) * (1.0 / D)
    sums = old + mean
    return rows - LEARN_RATE * grad * lax.rsqrt(sums), sums.T[0:1]


def kernel(
    v_ref, vs_ref, c_ref, cs_ref, hub_ref, hs_ref, src_ref, ctx_ref, neg_ref, cnt_ref,
    vo_ref, vso_ref, co_ref, cso_ref, gathered,
    hub_t, v_t, c_t, oh_hub, oh_src, oh_blk, chub_t, u_t, u2_t, w2, u2, pos_t, pu_t, live_u_t,
    q_parts, hist, grad_c, delta, parts, mid_rows, mid_sums, far, rx, rz, v_mid, block_out, block_in,
    send_sem, recv_sem,
):
    narrow = lax.axis_index("narrow")
    wide = lax.axis_index("wide")
    n_wide = lax.axis_size("wide")
    x = narrow // RING
    z = lax.rem(narrow, RING)

    def at(xx, zz):
        return {"narrow": lax.rem(xx, RING) * RING + lax.rem(zz, RING)}

    x_right, x_left = at(x + 1, z), at(x + 3, z)
    z_right, z_left = at(x, z + 1), at(x, z + 3)
    x_far, z_far = at(x + 2, z), at(x, z + 2)
    w_next = {"wide": lax.rem(wide + 1, n_wide)}
    w_prev = {"wide": lax.rem(wide + n_wide - 1, n_wide)}

    barrier = pltpu.get_barrier_semaphore()
    for other in (x_right, x_left, x_far, z_right, z_left, z_far, w_next, w_prev):
        pl.semaphore_signal(barrier, inc=1, device_id=other, device_id_type=MESH)

    started = []

    def send(src, dst, device):
        slot = len(started)
        copy = pltpu.make_async_remote_copy(
            src_ref=src,
            dst_ref=dst,
            send_sem=send_sem.at[slot],
            recv_sem=recv_sem.at[slot],
            device_id=device,
            device_id_type=MESH,
        )
        copy.start()
        started.append(copy)
        return copy

    def hub_base(zz, xx):
        return pl.multiple_of(
            lax.rem(zz, RING) * (RING * BLOCK) + lax.rem(xx, RING) * BLOCK, BLOCK
        )


    def prepare_hub():
        for part in range(RING):
            rows = pl.ds(part * ROWS, ROWS)
            hi, lo = split(hub_ref[rows, :].T)
            hub_t[0:D, rows] = hi
            hub_t[D : 2 * D, rows] = lo

    def gather_hub(s):
        def body(tile, carry):
            cols = pl.ds(pl.multiple_of(tile * 256, 256), 256)
            hot = one_hot(ctx_ref[s : s + 1, cols] - ROWS, HUB)
            oh_hub[s, :, cols] = hot
            got = mm(hub_t[...], hot)
            chub_t[:, cols] = got[0:D] + got[D : 2 * D]
            return carry

        lax.fori_loop(0, EDGES // 256, body, 0)

    def live_row(s):
        slot = lax.broadcasted_iota(jnp.int32, (1, EDGES), 1)
        return jnp.where(slot < cnt_ref[0, s], 1.0, 0.0)

    def positive(score, live):
        return (0.5 * jnp.tanh(0.5 * score) - 0.5) * live

    def put_rows(ref, value_t):
        for part in range(EDGES // 256):
            hi, lo = split(value_t[:, part * 256 : (part + 1) * 256].T)
            rows = pl.ds(part * 256, 256)
            ref[rows, 0:D] = hi
            ref[rows, D : 2 * D] = lo

    def gather_vertices(s, rows):
        oh_src[...] = one_hot(src_ref[s : s + 1, :], ROWS)
        hi, lo = split(rows.T)
        v_t[0:D, :] = hi
        v_t[D : 2 * D, :] = lo
        got = mm(v_t[...], oh_src[...])
        u2_t[...] = got.astype(BF16)
        u_t[...] = got[0:D] + got[D : 2 * D]

    def hub_gradient(s):
        u = u_t[...]
        score = jnp.sum(u * chub_t[...], axis=0, keepdims=True)
        put_rows(w2, u * positive(score, live_row(s)))

    def hub_piece(s, k):
        rows = pl.ds(hub_base(z + ORDER[k], 0), ROWS)
        got = mm(oh_hub[s, rows, :], w2[...])
        delta[s, rows, :] = got[:, 0:D] + got[:, D : 2 * D]

    def block_edges(s, block):
        live = live_row(s)
        oh_blk[...] = one_hot(ctx_ref[s : s + 1, :], ROWS)
        hi, lo = split(block.T)
        c_t[0:D, :] = hi
        c_t[D : 2 * D, :] = lo
        got = mm(c_t[...], oh_blk[...])
        c_all = chub_t[...] + got[0:D] + got[D : 2 * D]
        u = u_t[...]
        score = jnp.sum(u * c_all, axis=0, keepdims=True)
        p = positive(score, live)
        pos_t[...] = p * c_all
        pu_t[...] = u * p
        live_u_t[...] = u * live

    def count_negatives(s):
        for b in range(EDGES // BATCH):
            hot = one_hot(neg_ref[s, b : b + 1, :], ROWS)
            hist[s, b] = mm(hot, jnp.ones((hot.shape[1], D), BF16))

    def batch(s, b, block):
        cols = pl.ds(b * BATCH, BATCH)
        hi, lo = split(0.5 * block)
        both = u2_t[:, cols]
        half_score = mm(jnp.concatenate([hi, hi], axis=1), both) + mm(lo, both[0:D])
        q_hi, q_lo = split(0.5 * jnp.tanh(half_score) + 0.5)
        q_parts[0, :, cols] = q_hi
        q_parts[1, :, cols] = q_lo
        weighted = (NEG_WEIGHT * hist[s, b]) * block
        m_hi, m_lo = split(weighted.T)
        pulled = mm(jnp.concatenate([m_hi, m_lo], axis=0), q_hi)
        pulled = pulled[0:D] + pulled[D : 2 * D] + mm(m_hi, q_lo)
        slot = lax.broadcasted_iota(jnp.int32, (1, BATCH), 1) + b * BATCH
        pos_t[:, cols] += pulled * jnp.where(slot < cnt_ref[0, s], 1.0, 0.0)

    def block_gradient(s):
        put_rows(u2, pu_t[...])
        got = mm(oh_blk[...], u2[...])
        total = got[:, 0:D] + got[:, D : 2 * D]
        put_rows(u2, live_u_t[...])
        for b in range(EDGES // BATCH):
            cols = pl.ds(b * BATCH, BATCH)
            u_rows = u2[cols, :]
            got = mm(q_parts[0, :, cols], u_rows)
            got = got[:, 0:D] + got[:, D : 2 * D] + mm(q_parts[1, :, cols], u_rows[:, 0:D])
            total = total + (NEG_WEIGHT * hist[s, b]) * got
        grad_c[...] = total

    def update_vertices(read, write):
        put_rows(w2, pos_t[...])
        got = mm(oh_src[...], w2[...])
        grad = got[:, 0:D] + got[:, D : 2 * D]
        for part in range(ROWS // BLOCK):
            rows = slice(part * BLOCK, (part + 1) * BLOCK)
            write(part, *adagrad_block(*read(part), grad[rows]))

    def update_block(read, write):
        for part in range(ROWS // BLOCK):
            rows = slice(part * BLOCK, (part + 1) * BLOCK)
            write(part, *adagrad_block(*read(part), grad_c[rows, :]))


    ring_copies = {}
    cross_copies = {}

    def base_of(part, along, across):
        if part[3] == "x":
            return hub_base(z + across, x + along) + part[1]
        return hub_base(z + along, x + across) + part[1]

    def device_of(part, along, across):
        return at(x + along, z + across) if part[3] == "x" else at(x + across, z + along)

    def ring_first(part, k):
        s, lo, n, _ = part
        half = n // 2
        right, left = device_of(part, 1, 0), device_of(part, 3, 0)
        two, one, back = (base_of(part, d, ORDER[k]) for d in (2, 1, 3))
        d = delta.at[s]

        def land(way, kind):
            return rx.at[s, k, way, kind].at[pl.ds(lo // 2, half)]

        if k == 0 and part in DIRECT:
            ring_copies[part, k] = [
                send(d.at[pl.ds(two, n)], far.at[s, 0].at[pl.ds(lo, n)], device_of(part, 2, 0)),
                send(d.at[pl.ds(one, n)], far.at[s, 1].at[pl.ds(lo, n)], right),
                send(d.at[pl.ds(back, n)], far.at[s, 2].at[pl.ds(lo, n)], left),
            ]
            return
        ring_copies[part, k] = [
            send(d.at[pl.ds(two, half)], land(0, 0), right),
            send(d.at[pl.ds(two + half, half)], land(1, 0), left),
            send(d.at[pl.ds(one + half, half)], land(0, 1), right),
            send(d.at[pl.ds(back, half)], land(1, 1), left),
        ]

    def ring_second(part, k):
        if k == 0 and part in DIRECT:
            return
        s, lo, n, _ = part
        half = n // 2
        one, back = (base_of(part, d, ORDER[k]) for d in (1, 3))
        d = delta.at[s]
        got = pl.ds(lo // 2, half)
        copies = ring_copies[part, k]
        rows = pl.ds(one, half)
        copies[0].wait_recv()
        delta[s, rows, :] += rx[s, k, 0, 0, got, :]
        copies.append(send(d.at[rows], rx.at[s, k, 0, 2].at[got], device_of(part, 1, 0)))
        rows = pl.ds(back + half, half)
        copies[1].wait_recv()
        delta[s, rows, :] += rx[s, k, 1, 0, got, :]
        copies.append(send(d.at[rows], rx.at[s, k, 1, 2].at[got], device_of(part, 3, 0)))

    def ring_last(part, k):
        s, lo, n, _ = part
        half = n // 2
        mine = base_of(part, 0, ORDER[k])
        copies = ring_copies[part, k]
        whole = pl.ds(lo, n)
        if k == 0 and part in DIRECT:
            total = delta[s, pl.ds(mine, n), :]
            for way in (1, 2, 0):
                copies[way].wait_recv()
                total = total + far[s, way, whole, :]
            parts[s, k, whole, :] = total
        else:
            got = pl.ds(lo // 2, half)
            for copy in copies[2:]:
                copy.wait_recv()
            parts[s, k, pl.ds(lo, half), :] = (
                delta[s, pl.ds(mine, half), :] + rx[s, k, 0, 2, got, :] + rx[s, k, 1, 1, got, :]
            )
            parts[s, k, pl.ds(lo + half, half), :] = (
                delta[s, pl.ds(mine + half, half), :]
                + rx[s, k, 0, 1, got, :]
                + rx[s, k, 1, 2, got, :]
            )
        if ORDER[k]:
            cross_copies[part, k] = send(
                parts.at[s, k].at[whole], rz.at[s, k].at[whole], device_of(part, 0, ORDER[k])
            )

    def reduced(part):
        s, lo, n, _ = part
        whole = pl.ds(lo, n)
        total = parts[s, RING - 1, whole, :]
        for k in (1, 2, 0):
            cross_copies[part, k].wait_recv()
            total = total + rz[s, k, whole, :]
        return total

    def each(function, parts_, pieces=(0, 1, 2, 3)):
        for part in parts_:
            for k in pieces:
                function(part, k)


    def slot_of(zz, xx):
        return lax.rem(zz, RING) * RING + lax.rem(xx, RING)

    me = slot_of(z, x)
    gathers = {}

    def spread(h, slot, device, lo=0, n=PACK):
        block = gathered.at[slot, h].at[pl.ds(lo, n)]
        return send(block, block, device)

    def gather_first(h):
        rows = pl.ds(h * HALF, HALF)
        grad = jnp.concatenate([reduced(part) for part in SECOND[h]], axis=0)
        sums = mid_sums[rows, :] + jnp.sum(grad * grad, axis=1, keepdims=True) * (1.0 / D)
        gathered[me, h, 0:HALF, :] = mid_rows[rows, :] - LEARN_RATE * grad * lax.rsqrt(sums)
        none = jnp.zeros((HALF, D), F32)
        column = jnp.concatenate([sums, none] if h == 0 else [none, sums], axis=0)
        gathered[me, h, HALF:PACK, :] = column.T[0:8]
        z_l, z_r = spread(h, me, z_left), spread(h, me, z_right)
        z_two = spread(h, me, z_far)
        gathers[h] = {
            "z": (z_r, z_l, z_two),
            0: (spread(h, me, x_right), spread(h, me, x_left)),
            "last": [],
        }

    def gather_near(h):
        z_r, z_l, _ = gathers[h]["z"]
        for copy, dz in ((z_r, 3), (z_l, 1)):
            copy.wait_recv()
            slot = slot_of(z + dz, x)
            gathers[h][dz] = (spread(h, slot, x_right), spread(h, slot, x_left))

    def gather_far(h):
        gathers[h]["z"][2].wait_recv()
        slot = slot_of(z + 2, x)
        for device in (x_far, x_right, x_left):
            gathers[h]["last"].append(spread(h, slot, device))

    def forward(h, dz):
        right, left = gathers[h][dz]
        last = gathers[h]["last"]
        right.wait_recv()
        last.append(spread(h, slot_of(z + dz, x + 3), x_right, 0, HALF // 2))
        left.wait_recv()
        last.append(spread(h, slot_of(z + dz, x + 1), x_left, HALF // 2, PACK - HALF // 2))


    def part_of(part):
        return pl.ds(part * BLOCK, BLOCK)

    def read_vertex(part):
        return v_ref[part_of(part), :], vs_ref[:, part_of(part)]

    def write_vertex_mid(part, rows, sums):
        v_mid[part_of(part), :] = rows
        vso_ref[:, part_of(part)] = sums

    def read_block(part):
        return c_ref[part_of(part), :], cs_ref[:, part_of(part)]

    def write_block_out(part, rows, sums):
        block_out[part_of(part), :] = rows
        block_out[ROWS + part : ROWS + part + 1, :] = sums

    def read_vertex_mid(part):
        return v_mid[part_of(part), :], vso_ref[:, part_of(part)]

    def write_vertex(part, rows, sums):
        vo_ref[part_of(part), :] = rows
        vso_ref[:, part_of(part)] = sums

    def read_block_in(part):
        return block_in[part_of(part), :], block_in[ROWS + part : ROWS + part + 1, :]

    def write_block(part, rows, sums):
        co_ref[part_of(part), :] = rows
        cso_ref[:, part_of(part)] = sums

    prepare_hub()
    gather_hub(0)
    gather_vertices(0, v_ref[...])
    hub_gradient(0)
    pl.semaphore_wait(barrier, 8)
    for k in range(RING):
        hub_piece(0, k)
        each(ring_first, [p for p in FIRST if p[3] == "x"], [k])
    each(ring_first, [p for p in FIRST if p[3] == "z"])
    block_edges(0, c_ref[...])
    count_negatives(0)
    batch(0, 0, c_ref[...])
    each(ring_second, FIRST)
    batch(0, 1, c_ref[...])
    each(ring_last, FIRST, [0])
    update_vertices(read_vertex, write_vertex_mid)


    gather_hub(1)
    each(ring_last, FIRST, [1, 2, 3])
    gather_vertices(1, v_mid[...])
    hub_gradient(1)
    for k in range(RING):
        hub_piece(1, k)
        each(ring_first, [p for p in SECOND[0] if p[3] == "x"], [k])
    each(ring_first, [p for p in SECOND[0] if p[3] == "z"])
    each(ring_first, SECOND[1])

    block_gradient(0)
    update_block(read_block, write_block_out)
    for part in range(ROWS // BLOCK, 8):
        block_out[ROWS + part : ROWS + part + 1, :] = jnp.zeros((1, D), F32)
    shift = send(block_out, block_in, w_next)
    count_negatives(1)
    each(ring_second, SECOND[0])
    each(ring_last, SECOND[0], [0])
    each(ring_second, SECOND[1])
    each(ring_last, SECOND[1], [0])
    own = pl.ds(hub_base(z, x), BLOCK)
    old = jnp.broadcast_to(hs_ref[:, own], (BLOCK, D)).T
    grad = jnp.concatenate([reduced(part) for part in FIRST], axis=0)
    sums = old + jnp.sum(grad * grad, axis=1, keepdims=True) * (1.0 / D)
    mid_sums[...] = sums
    mid_rows[...] = hub_ref[own, :] - LEARN_RATE * grad * lax.rsqrt(sums)
    shift.wait_recv()
    block_edges(1, block_in[0:ROWS, :])
    each(ring_last, SECOND[0], [1, 2, 3])
    batch(1, 0, block_in[0:ROWS, :])
    each(ring_last, SECOND[1], [1, 2, 3])
    batch(1, 1, block_in[0:ROWS, :])
    gather_first(0)
    update_vertices(read_vertex_mid, write_vertex)
    gather_first(1)
    block_gradient(1)
    update_block(read_block_in, write_block)
    gather_near(0)
    forward(0, 0)
    gather_far(0)
    gather_near(1)
    forward(0, 3)
    forward(0, 1)
    forward(1, 0)
    gather_far(1)
    forward(1, 3)
    forward(1, 1)
    for h in range(2):
        for copy in gathers[h]["last"]:
            copy.wait_recv()
    for copy in started:
        copy.wait_send()


def place(vo, vso, co, cso, rows, vo_ref, vso_ref, co_ref, cso_ref, ho_ref, hso_ref, sem):
    copies = [
        pltpu.make_async_copy(
            rows.at[pl.ds(i * RING, RING), :, pl.ds(0, HALF), :],
            ho_ref.at[pl.ds(i * RING, RING)],
            sem.at[i],
        )
        for i in range(RING)
    ]
    copies.append(pltpu.make_async_copy(vo, vo_ref, sem.at[RING]))
    copies.append(pltpu.make_async_copy(co, co_ref, sem.at[RING + 1]))
    for copy in copies:
        copy.start()
    vso_ref[...] = vso[...]
    cso_ref[...] = cso[...]
    for block in range(RING * RING):
        hso_ref[:, block * BLOCK : (block + 1) * BLOCK] = (
            rows[block, 0, HALF : HALF + 1, :] + rows[block, 1, HALF : HALF + 1, :]
        )
    for copy in copies:
        copy.wait()


PARTS = FIRST + SECOND[0] + SECOND[1]
N_COPIES = sum(27 - 3 * (p in DIRECT) for p in PARTS) + 1 + 2 * (3 + 3 * 4 + 3)


def per_device(
    vertex, vertex_state, context, context_state, hub, hub_state, edge_src, edge_ctx, negatives, counts
):
    vmem = pl.BlockSpec(memory_space=pltpu.VMEM)
    inner = (
        pltpu.VMEM((ROWS, D), F32),
        pltpu.VMEM((1, ROWS), F32),
        pltpu.VMEM((ROWS, D), F32),
        pltpu.VMEM((1, ROWS), F32),
        pltpu.VMEM((RING * RING, 2, PACK, D), F32),
    )
    shapes = (
        jax.ShapeDtypeStruct((ROWS, D), F32),
        jax.ShapeDtypeStruct((1, ROWS), F32),
        jax.ShapeDtypeStruct((ROWS, D), F32),
        jax.ShapeDtypeStruct((1, ROWS), F32),
        jax.ShapeDtypeStruct((RING * RING, 2, HALF, D), F32),
        jax.ShapeDtypeStruct((1, HUB), F32),
    )
    scratch = [
        pltpu.VMEM((2 * D, HUB), BF16),
        pltpu.VMEM((2 * D, ROWS), BF16),
        pltpu.VMEM((2 * D, ROWS), BF16),
        pltpu.VMEM((2, HUB, EDGES), BF16),
        pltpu.VMEM((ROWS, EDGES), BF16),
        pltpu.VMEM((ROWS, EDGES), BF16),
        pltpu.VMEM((D, EDGES), F32),
        pltpu.VMEM((D, EDGES), F32),
        pltpu.VMEM((2 * D, EDGES), BF16),
        pltpu.VMEM((EDGES, 2 * D), BF16),
        pltpu.VMEM((EDGES, 2 * D), BF16),
        pltpu.VMEM((D, EDGES), F32),
        pltpu.VMEM((D, EDGES), F32),
        pltpu.VMEM((D, EDGES), F32),
        pltpu.VMEM((2, ROWS, EDGES), BF16),
        pltpu.VMEM((2, 2, ROWS, D), F32),
        pltpu.VMEM((ROWS, D), F32),
        pltpu.VMEM((2, HUB, D), F32),
        pltpu.VMEM((2, RING, BLOCK, D), F32),
        pltpu.VMEM((BLOCK, D), F32),
        pltpu.VMEM((BLOCK, D), F32),
        pltpu.VMEM((2, 3, BLOCK, D), F32),
        pltpu.VMEM((2, RING, 2, 3, HALF, D), F32),
        pltpu.VMEM((2, RING - 1, BLOCK, D), F32),
        pltpu.VMEM((ROWS, D), F32),
        pltpu.VMEM((ROWS + 8, D), F32),
        pltpu.VMEM((ROWS + 8, D), F32),
        pltpu.SemaphoreType.DMA((N_COPIES,)),
        pltpu.SemaphoreType.DMA((N_COPIES,)),
    ]
    found = pl.pallas_call(
        kernel,
        out_shape=inner,
        in_specs=[vmem] * 9 + [pl.BlockSpec(memory_space=pltpu.SMEM)],
        out_specs=[vmem] * 5,
        scratch_shapes=scratch,
        compiler_params=pltpu.CompilerParams(
            collective_id=0, has_side_effects=True, vmem_limit_bytes=58 * 1024 * 1024
        ),
        name="skipgram_window",
    )(
        vertex[0, 0],
        vertex_state[0],
        context[0, 0],
        context_state[0],
        hub[0],
        hub_state,
        edge_src[0, 0],
        edge_ctx[0, 0],
        negatives[0, 0],
        counts[0],
    )
    hbm = pl.BlockSpec(memory_space=pl.ANY)
    out = pl.pallas_call(
        place,
        out_shape=shapes,
        in_specs=[vmem] * 5,
        out_specs=(hbm, vmem, hbm, vmem, hbm, vmem),
        scratch_shapes=[pltpu.SemaphoreType.DMA((RING + 2,))],
        compiler_params=pltpu.CompilerParams(vmem_limit_bytes=4 * 1024 * 1024),
        name="place_results",
    )(*found)
    return (
        out[0][None, None],
        out[1][None],
        out[2][None, None],
        out[3][None],
        out[4].reshape(1, HUB, D),
        out[5],
    )


def solution(mesh):
    narrow_wide = lambda n: P("narrow", "wide", *([None] * n))
    in_specs = (
        narrow_wide(2),
        narrow_wide(1),
        narrow_wide(2),
        narrow_wide(1),
        P("wide", None, None),
        P("wide", None),
        narrow_wide(2),
        narrow_wide(2),
        narrow_wide(3),
        narrow_wide(1),
    )
    out_specs = (
        narrow_wide(2),
        narrow_wide(1),
        narrow_wide(2),
        narrow_wide(1),
        P("wide", None, None),
        P("wide", None),
    )
    return jax.shard_map(
        per_device, mesh=mesh, in_specs=in_specs, out_specs=out_specs, check_vma=False
    )
```
